32 devices in a mesh: line: 4 (over y, x), cross: 8 (over z, core).
Axes of the slice: x: 2, y: 2, z: 4, core: 2. Of those that a mesh axis runs over, the one named last changes fastest.
Arguments:
- velocity: float32 [3, 512, 64, 256], P(None, 'line', 'cross'), may hold values from -6 to 6
Outputs:
- advection: float32 [3, 512, 64, 256], P(None, 'line', 'cross')
- x_derivative: float32 [3, 512, 64, 256], P(None, 'line', 'cross')
The draws below stay inside these ranges and needn't reach their ends.
All inputs are finite; a program needn't handle non-finite values.
Results may differ from the reference program's by a relative error of at most 0.0001.
Values sent between devices are 32-bit elements; how exact they have to be, the bound alone decides.
A program may use at most 128 MiB of HBM per device.

```python
import math
import jax
import jax.numpy as jnp

NX = 512
NZ = 256
NY = 64


def shard_levels(own_key, shape, shards, low, top_value):
    def one(position, blocks):
        heights = jax.random.uniform(jax.random.fold_in(jax.random.fold_in(own_key, 6), position), (blocks,), jnp.float32, low / len(shards), top_value / len(shards))
        return jnp.repeat(jnp.exp(heights), shape[position] // blocks).reshape((-1,) + (1,) * (len(shape) - position - 1))

    loudness = one(*shards[0])
    for cut in shards[1:]:
        loudness = loudness * one(*cut)
    return loudness


def noise(own_key, shape, deviation, bound, split=(), held_as=jnp.bfloat16):
    values = deviation * jax.random.normal(own_key, shape, jnp.float32)
    if split:
        values = values * shard_levels(own_key, shape, split, -0.22, 0.18)
    return jnp.clip(values, -bound, bound).astype(held_as)


def setup_inputs(seed: int = 0) -> dict:
    seeds = jax.random.split(jax.random.key(seed), 2)
    velocity = noise(seeds[0], (3, NX, NY, NZ), 1.0, 6.0, ((1, 4), (2, 8)), jnp.float32)
    return {"velocity": velocity}


ALPHA = 1.0 / 3.0
COEF_A = 14.0 / 9.0
COEF_B = 1.0 / 9.0


def explicit_sixth(field, axis):
    total = 45.0 * (jnp.roll(field, -1, axis) - jnp.roll(field, 1, axis))
    total = total - 9.0 * (jnp.roll(field, -2, axis) - jnp.roll(field, 2, axis))
    total = total + (jnp.roll(field, -3, axis) - jnp.roll(field, 3, axis))
    return total / 60.0


def compact_x(field):
    waves = 2.0 * math.pi * jnp.arange(NX // 2 + 1).astype(jnp.float32) / NX
    factor = (COEF_A * jnp.sin(waves) + 0.5 * COEF_B * jnp.sin(2.0 * waves)) / (1.0 + 2.0 * ALPHA * jnp.cos(waves))
    spectrum = jnp.fft.rfft(field, axis=0)
    result = jnp.fft.irfft(spectrum * (1j * factor)[:, None, None], n=NX, axis=0)
    return result.astype(field.dtype)


def reference(velocity):
    speed_u, speed_v, speed_w = velocity[0], velocity[1], velocity[2]
    advected = []
    derived = []
    for comp in range(3):
        field = velocity[comp]
        along_x = compact_x(field)
        along_y = explicit_sixth(field, 1)
        along_z = explicit_sixth(field, 2)
        advected.append(-(speed_u * along_x + speed_v * along_y + speed_w * along_z))
        derived.append(along_x)
    return jnp.stack(advected), jnp.stack(derived)
```

```python
import functools
import math

import jax
import jax.numpy as jnp
from jax import lax
from jax.experimental import pallas as pl
from jax.experimental.pallas import tpu as pltpu
from jax.sharding import PartitionSpec as P

MESH = pl.DeviceIdType.MESH
ALPHA = 1.0 / 3.0
NEAR = 7.0 / 9.0
FAR = 1.0 / 36.0
ROOT = (math.sqrt(1.0 - 4.0 * ALPHA * ALPHA) - 1.0) / (2.0 * ALPHA)
SCALE = 1.0 + ROOT * ROOT
STENCIL = (45.0 / 60.0, -9.0 / 60.0, 1.0 / 60.0)
WIDTH = 3
CHUNKS = 8
COMPS = 3


def kernel(
    lines,
    tiles,
    vel,
    adv,
    gx,
    vx,
    halo,
    ends,
    beside,
    power,
    in_sem,
    y_send,
    y_recv,
    x_send,
    x_recv,
    e_send,
    e_recv,
):
    seg = vel.shape[1]
    rows = vel.shape[2]
    chunk = seg // CHUNKS
    line = lax.axis_index("line")
    tile = lax.axis_index("cross")
    ahead = (lax.rem(line + 1, lines), tile)
    behind = (lax.rem(line + lines - 1, lines), tile)
    above = (line, lax.rem(tile + 1, tiles))
    below = (line, lax.rem(tile + tiles - 1, tiles))

    local = pltpu.make_async_copy(vel, vx.at[:, 2 : 2 + seg], in_sem)
    local.start()

    barrier = pltpu.get_barrier_semaphore()
    for device in (above, below, ahead, behind):
        pl.semaphore_signal(barrier, inc=1, device_id=device, device_id_type=MESH)
    pl.semaphore_wait(barrier, 4)

    def remote(src, dst, send, recv, device):
        return pltpu.make_async_remote_copy(
            src_ref=src,
            dst_ref=dst,
            send_sem=send,
            recv_sem=recv,
            device_id=device,
            device_id_type=MESH,
        )

    x_copies = [
        remote(vel.at[:, seg - 2 : seg], vx.at[:, 0:2], x_send.at[0], x_recv.at[0], ahead),
        remote(vel.at[:, 0:2], vx.at[:, seg + 2 : seg + 4], x_send.at[1], x_recv.at[1], behind),
    ]
    for copy in x_copies:
        copy.start()

    y_copies = []
    for part in range(CHUNKS):
        planes = slice(part * chunk, (part + 1) * chunk)
        head = slice(0, WIDTH)
        tail = slice(rows - WIDTH, rows)
        pair = (
            remote(
                vel.at[:, planes, tail],
                halo.at[:, planes, tail],
                y_send.at[0, part],
                y_recv.at[0, part],
                above,
            ),
            remote(
                vel.at[:, planes, head],
                halo.at[:, planes, head],
                y_send.at[1, part],
                y_recv.at[1, part],
                below,
            ),
        )
        for copy in pair:
            copy.start()
        y_copies.append(pair)

    def fill(i, value):
        power[i] = value
        return value * ROOT

    lax.fori_loop(0, seg, fill, jnp.float32(ROOT))

    local.wait()
    for copy in x_copies:
        copy.wait()

    zero = jnp.zeros((COMPS,) + vel.shape[2:], jnp.float32)

    def forward(i, before):
        near = vx[:, i + 3] - vx[:, i + 1]
        far = vx[:, i + 4] - vx[:, i]
        now = (NEAR * near + FAR * far) + ROOT * before
        gx[:, i] = now
        return now

    ends[0] = lax.fori_loop(0, seg, forward, zero, unroll=4)

    def backward(k, after):
        i = seg - 1 - k
        now = SCALE * gx[:, i] + ROOT * after
        gx[:, i] = now
        return now

    ends[1] = lax.fori_loop(0, seg, backward, zero, unroll=4)

    e_copies = [
        remote(ends.at[0], beside.at[0], e_send.at[0], e_recv.at[0], ahead),
        remote(ends.at[1], beside.at[1], e_send.at[1], e_recv.at[1], behind),
    ]
    for copy in e_copies:
        copy.start()

    depth = vel.shape[3]

    def along_z(i, carry):
        w = vx[2, i + 2]
        for c in range(COMPS):
            field = vx[c, i + 2]
            total = None
            for k, weight in enumerate(STENCIL, 1):
                diff = pltpu.roll(field, depth - k, 1) - pltpu.roll(field, k, 1)
                total = weight * diff if total is None else total + weight * diff
            adv[c, i] = w * total
        return carry

    lax.fori_loop(0, seg, along_z, 0, unroll=2)

    for copy in e_copies:
        copy.wait()

    gain = SCALE / (1.0 - ROOT * ROOT)
    left = gain * beside[0]
    right = beside[1] + (gain * ROOT) * ends[0] - (gain * ROOT ** (seg + 1)) * beside[0]

    def along_x(i, carry):
        u = vx[0, i + 2]
        for c in range(COMPS):
            value = gx[c, i] + (power[i] * left[c] + power[seg - 1 - i] * right[c])
            gx[c, i] = value
            adv[c, i] = adv[c, i] + u * value
        return carry

    lax.fori_loop(0, seg, along_x, 0, unroll=2)

    row = lax.broadcasted_iota(jnp.int32, vel.shape[2:], 0)

    def along_y(i, carry):
        v = vx[1, i + 2]
        for c in range(COMPS):
            field = vx[c, i + 2]
            other = halo[c, i]
            total = None
            for k, weight in enumerate(STENCIL, 1):
                up = pltpu.roll(jnp.where(row < k, other, field), rows - k, 0)
                down = pltpu.roll(jnp.where(row >= rows - k, other, field), k, 0)
                diff = up - down
                total = weight * diff if total is None else total + weight * diff
            adv[c, i] = -(adv[c, i] + v * total)
        return carry

    for part in range(CHUNKS):
        for copy in y_copies[part]:
            copy.wait_recv()
        lax.fori_loop(part * chunk, (part + 1) * chunk, along_y, 0, unroll=2)
    for pair in y_copies:
        for copy in pair:
            copy.wait_send()


def on_device(lines, tiles, velocity):
    comps, seg, rows, depth = velocity.shape
    plane = (comps, rows, depth)
    shape = jax.ShapeDtypeStruct(velocity.shape, jnp.float32)
    adv, gx = pl.pallas_call(
        functools.partial(kernel, lines, tiles),
        out_shape=(shape, shape),
        in_specs=[pl.BlockSpec(memory_space=pl.ANY)],
        out_specs=(
            pl.BlockSpec(memory_space=pltpu.VMEM),
            pl.BlockSpec(memory_space=pltpu.VMEM),
        ),
        scratch_shapes=[
            pltpu.VMEM((comps, seg + 4, rows, depth), jnp.float32),
            pltpu.VMEM(velocity.shape, jnp.float32),
            pltpu.VMEM((2,) + plane, jnp.float32),
            pltpu.VMEM((2,) + plane, jnp.float32),
            pltpu.SMEM((seg,), jnp.float32),
            pltpu.SemaphoreType.DMA,
            pltpu.SemaphoreType.DMA((2, CHUNKS)),
            pltpu.SemaphoreType.DMA((2, CHUNKS)),
            pltpu.SemaphoreType.DMA((2,)),
            pltpu.SemaphoreType.DMA((2,)),
            pltpu.SemaphoreType.DMA((2,)),
            pltpu.SemaphoreType.DMA((2,)),
        ],
        compiler_params=pltpu.CompilerParams(
            collective_id=0, has_side_effects=True, vmem_limit_bytes=40 * 1024 * 1024
        ),
    )(velocity)
    return adv, gx


def solution(mesh):
    spec = P(None, "line", "cross", None)
    return jax.shard_map(
        functools.partial(on_device, mesh.shape["line"], mesh.shape["cross"]),
        mesh=mesh,
        in_specs=(spec,),
        out_specs=(spec, spec),
        check_vma=False,
    )
```

```python
import functools
import math

import jax
import jax.numpy as jnp
from jax import lax
from jax.experimental import pallas as pl
from jax.experimental.pallas import tpu as pltpu
from jax.sharding import PartitionSpec as P

MESH = pl.DeviceIdType.MESH
ALPHA = 1.0 / 3.0
NEAR = 7.0 / 9.0
FAR = 1.0 / 36.0
ROOT = (math.sqrt(1.0 - 4.0 * ALPHA * ALPHA) - 1.0) / (2.0 * ALPHA)
SCALE = 1.0 + ROOT * ROOT
STENCIL = (45.0 / 60.0, -9.0 / 60.0, 1.0 / 60.0)
WIDTH = 3
CHUNKS = 8
COMPS = 3
PIECES = 4


def kernel(
    lines,
    tiles,
    vel,
    adv,
    gx,
    vx,
    halo,
    ends,
    beside,
    power,
    in_sem,
    y_send,
    y_recv,
    x_send,
    x_recv,
    e_send,
    e_recv,
):
    seg = vel.shape[1]
    rows = vel.shape[2]
    chunk = seg // CHUNKS
    line = lax.axis_index("line")
    tile = lax.axis_index("cross")
    ahead = (lax.rem(line + 1, lines), tile)
    behind = (lax.rem(line + lines - 1, lines), tile)
    above = (line, lax.rem(tile + 1, tiles))
    below = (line, lax.rem(tile + tiles - 1, tiles))

    local = pltpu.make_async_copy(vel, vx.at[:, 2 : 2 + seg], in_sem)
    local.start()

    barrier = pltpu.get_barrier_semaphore()
    for device in (above, below, ahead, behind):
        pl.semaphore_signal(barrier, inc=1, device_id=device, device_id_type=MESH)
    pl.semaphore_wait(barrier, 4)

    def remote(src, dst, send, recv, device):
        return pltpu.make_async_remote_copy(
            src_ref=src,
            dst_ref=dst,
            send_sem=send,
            recv_sem=recv,
            device_id=device,
            device_id_type=MESH,
        )

    x_copies = [
        remote(vel.at[:, seg - 2 : seg], vx.at[:, 0:2], x_send.at[0], x_recv.at[0], ahead),
        remote(vel.at[:, 0:2], vx.at[:, seg + 2 : seg + 4], x_send.at[1], x_recv.at[1], behind),
    ]
    for copy in x_copies:
        copy.start()

    y_copies = []
    for part in range(CHUNKS):
        planes = slice(part * chunk, (part + 1) * chunk)
        head = slice(0, WIDTH)
        tail = slice(rows - WIDTH, rows)
        pair = (
            remote(
                vel.at[:, planes, tail],
                halo.at[:, planes, tail],
                y_send.at[0, part],
                y_recv.at[0, part],
                above,
            ),
            remote(
                vel.at[:, planes, head],
                halo.at[:, planes, head],
                y_send.at[1, part],
                y_recv.at[1, part],
                below,
            ),
        )
        for copy in pair:
            copy.start()
        y_copies.append(pair)

    def fill(i, value):
        power[i] = value
        return value * ROOT

    lax.fori_loop(0, seg, fill, jnp.float32(ROOT))

    local.wait()
    for copy in x_copies:
        copy.wait()

    zero = jnp.zeros((COMPS,) + vel.shape[2:], jnp.float32)

    def forward(i, before):
        near = vx[:, i + 3] - vx[:, i + 1]
        far = vx[:, i + 4] - vx[:, i]
        now = (NEAR * near + FAR * far) + ROOT * before
        gx[:, i] = now
        return now

    ends[0] = lax.fori_loop(0, seg, forward, zero, unroll=4)

    def backward(k, after):
        i = seg - 1 - k
        now = SCALE * gx[:, i] + ROOT * after
        gx[:, i] = now
        return now

    ends[1] = lax.fori_loop(0, seg, backward, zero, unroll=4)

    e_copies = [
        remote(ends.at[0], beside.at[0], e_send.at[0], e_recv.at[0], ahead),
        remote(ends.at[1], beside.at[1], e_send.at[1], e_recv.at[1], behind),
    ]
    for copy in e_copies:
        copy.start()

    depth = vel.shape[3]

    def along_z(i, carry):
        w = vx[2, i + 2]
        for c in range(COMPS):
            field = vx[c, i + 2]
            total = None
            for k, weight in enumerate(STENCIL, 1):
                diff = pltpu.roll(field, depth - k, 1) - pltpu.roll(field, k, 1)
                total = weight * diff if total is None else total + weight * diff
            adv[c, i] = w * total
        return carry

    lax.fori_loop(0, seg, along_z, 0, unroll=2)

    for copy in e_copies:
        copy.wait()

    gain = SCALE / (1.0 - ROOT * ROOT)
    left = gain * beside[0]
    right = beside[1] + (gain * ROOT) * ends[0] - (gain * ROOT ** (seg + 1)) * beside[0]

    def along_x(i, carry):
        u = vx[0, i + 2]
        for c in range(COMPS):
            value = gx[c, i] + (power[i] * left[c] + power[seg - 1 - i] * right[c])
            gx[c, i] = value
            adv[c, i] = adv[c, i] + u * value
        return carry

    lax.fori_loop(0, seg, along_x, 0, unroll=2)

    row = lax.broadcasted_iota(jnp.int32, vel.shape[2:], 0)

    def along_y(i, carry):
        v = vx[1, i + 2]
        for c in range(COMPS):
            field = vx[c, i + 2]
            other = halo[c, i]
            total = None
            for k, weight in enumerate(STENCIL, 1):
                up = pltpu.roll(jnp.where(row < k, other, field), rows - k, 0)
                down = pltpu.roll(jnp.where(row >= rows - k, other, field), k, 0)
                diff = up - down
                total = weight * diff if total is None else total + weight * diff
            adv[c, i] = -(adv[c, i] + v * total)
        return carry

    for part in range(CHUNKS):
        for copy in y_copies[part]:
            copy.wait_recv()
        lax.fori_loop(part * chunk, (part + 1) * chunk, along_y, 0, unroll=2)
    for pair in y_copies:
        for copy in pair:
            copy.wait_send()


def place_out(adv_in, gx_in, adv_out, gx_out, sem):
    seg = adv_in.shape[1]
    piece = seg // PIECES
    copies = []
    for part in range(PIECES):
        planes = slice(part * piece, (part + 1) * piece)
        for which, (source, target) in enumerate(((adv_in, adv_out), (gx_in, gx_out))):
            copies.append(
                pltpu.make_async_copy(
                    source.at[:, planes], target.at[:, planes], sem.at[which, part]
                )
            )
    for copy in copies:
        copy.start()
    for copy in copies:
        copy.wait()


def on_device(lines, tiles, velocity):
    comps, seg, rows, depth = velocity.shape
    plane = (comps, rows, depth)
    shape = jax.ShapeDtypeStruct(velocity.shape, jnp.float32)
    adv, gx = pl.pallas_call(
        functools.partial(kernel, lines, tiles),
        out_shape=(shape, shape),
        in_specs=[pl.BlockSpec(memory_space=pltpu.HBM)],
        out_specs=(
            pl.BlockSpec(memory_space=pltpu.VMEM),
            pl.BlockSpec(memory_space=pltpu.VMEM),
        ),
        scratch_shapes=[
            pltpu.VMEM((comps, seg + 4, rows, depth), jnp.float32),
            pltpu.VMEM(velocity.shape, jnp.float32),
            pltpu.VMEM((2,) + plane, jnp.float32),
            pltpu.VMEM((2,) + plane, jnp.float32),
            pltpu.SMEM((seg,), jnp.float32),
            pltpu.SemaphoreType.DMA,
            pltpu.SemaphoreType.DMA((2, CHUNKS)),
            pltpu.SemaphoreType.DMA((2, CHUNKS)),
            pltpu.SemaphoreType.DMA((2,)),
            pltpu.SemaphoreType.DMA((2,)),
            pltpu.SemaphoreType.DMA((2,)),
            pltpu.SemaphoreType.DMA((2,)),
        ],
        compiler_params=pltpu.CompilerParams(
            collective_id=0, has_side_effects=True, vmem_limit_bytes=46 * 1024 * 1024
        ),
    )(velocity)
    return pl.pallas_call(
        place_out,
        out_shape=(shape, shape),
        in_specs=[pl.BlockSpec(memory_space=pltpu.VMEM)] * 2,
        out_specs=(pl.BlockSpec(memory_space=pltpu.HBM),) * 2,
        scratch_shapes=[pltpu.SemaphoreType.DMA((2, PIECES))],
        compiler_params=pltpu.CompilerParams(vmem_limit_bytes=24 * 1024 * 1024),
    )(adv, gx)


def solution(mesh):
    spec = P(None, "line", "cross", None)
    return jax.shard_map(
        functools.partial(on_device, mesh.shape["line"], mesh.shape["cross"]),
        mesh=mesh,
        in_specs=(spec,),
        out_specs=(spec, spec),
        check_vma=False,
    )
```

```python
import functools
import math

import jax
import jax.numpy as jnp
from jax import lax
from jax.experimental import pallas as pl
from jax.experimental.pallas import tpu as pltpu
from jax.sharding import PartitionSpec as P

MESH = pl.DeviceIdType.MESH
ALPHA = 1.0 / 3.0
NEAR = 7.0 / 9.0
FAR = 1.0 / 36.0
ROOT = (math.sqrt(1.0 - 4.0 * ALPHA * ALPHA) - 1.0) / (2.0 * ALPHA)
SCALE = 1.0 + ROOT * ROOT
STENCIL = (45.0 / 60.0, -9.0 / 60.0, 1.0 / 60.0)
WIDTH = 3
CHUNKS = 4
CUTS = (0, 32, 56, 61, 64)
COMPS = 3
PIECES = 4


def kernel(
    lines,
    tiles,
    vel,
    adv,
    gx,
    vx,
    halo,
    ends,
    beside,
    power,
    in_sem,
    y_send,
    y_recv,
    x_send,
    x_recv,
    e_send,
    e_recv,
):
    seg = vel.shape[1]
    rows = vel.shape[2]
    cuts = [seg * cut // CUTS[-1] for cut in CUTS]
    line = lax.axis_index("line")
    tile = lax.axis_index("cross")
    ahead = (lax.rem(line + 1, lines), tile)
    behind = (lax.rem(line + lines - 1, lines), tile)
    above = (line, lax.rem(tile + 1, tiles))
    below = (line, lax.rem(tile + tiles - 1, tiles))

    local = pltpu.make_async_copy(vel, vx.at[:, 2 : 2 + seg], in_sem)
    local.start()

    barrier = pltpu.get_barrier_semaphore()
    for device in (above, below, ahead, behind):
        pl.semaphore_signal(barrier, inc=1, device_id=device, device_id_type=MESH)
    pl.semaphore_wait(barrier, 4)

    def remote(src, dst, send, recv, device):
        return pltpu.make_async_remote_copy(
            src_ref=src,
            dst_ref=dst,
            send_sem=send,
            recv_sem=recv,
            device_id=device,
            device_id_type=MESH,
        )

    x_copies = [
        remote(vel.at[:, seg - 2 : seg], vx.at[:, 0:2], x_send.at[0], x_recv.at[0], ahead),
        remote(vel.at[:, 0:2], vx.at[:, seg + 2 : seg + 4], x_send.at[1], x_recv.at[1], behind),
    ]
    for copy in x_copies:
        copy.start()

    y_copies = []
    for part in range(CHUNKS):
        planes = slice(cuts[part], cuts[part + 1])
        head = slice(0, WIDTH)
        tail = slice(rows - WIDTH, rows)
        pair = (
            remote(
                vel.at[:, planes, tail],
                halo.at[:, planes, tail],
                y_send.at[0, part],
                y_recv.at[0, part],
                above,
            ),
            remote(
                vel.at[:, planes, head],
                halo.at[:, planes, head],
                y_send.at[1, part],
                y_recv.at[1, part],
                below,
            ),
        )
        for copy in pair:
            copy.start()
        y_copies.append(pair)

    def fill(i, value):
        power[i] = value
        return value * ROOT

    lax.fori_loop(0, seg, fill, jnp.float32(ROOT))

    local.wait()
    for copy in x_copies:
        copy.wait()

    zero = jnp.zeros((COMPS,) + vel.shape[2:], jnp.float32)

    def forward(i, before):
        near = vx[:, i + 3] - vx[:, i + 1]
        far = vx[:, i + 4] - vx[:, i]
        now = (NEAR * near + FAR * far) + ROOT * before
        gx[:, i] = now
        return now

    ends[0] = lax.fori_loop(0, seg, forward, zero, unroll=4)

    def backward(k, after):
        i = seg - 1 - k
        now = SCALE * gx[:, i] + ROOT * after
        gx[:, i] = now
        return now

    ends[1] = lax.fori_loop(0, seg, backward, zero, unroll=4)

    e_copies = [
        remote(ends.at[0], beside.at[0], e_send.at[0], e_recv.at[0], ahead),
        remote(ends.at[1], beside.at[1], e_send.at[1], e_recv.at[1], behind),
    ]
    for copy in e_copies:
        copy.start()

    depth = vel.shape[3]

    def along_z(i, carry):
        w = vx[2, i + 2]
        for c in range(COMPS):
            field = vx[c, i + 2]
            total = None
            for k, weight in enumerate(STENCIL, 1):
                diff = pltpu.roll(field, depth - k, 1) - pltpu.roll(field, k, 1)
                total = weight * diff if total is None else total + weight * diff
            adv[c, i] = w * total
        return carry

    lax.fori_loop(0, seg, along_z, 0, unroll=2)

    for copy in e_copies:
        copy.wait()

    gain = SCALE / (1.0 - ROOT * ROOT)
    left = gain * beside[0]
    right = beside[1] + (gain * ROOT) * ends[0] - (gain * ROOT ** (seg + 1)) * beside[0]

    def along_x(i, carry):
        u = vx[0, i + 2]
        for c in range(COMPS):
            value = gx[c, i] + (power[i] * left[c] + power[seg - 1 - i] * right[c])
            gx[c, i] = value
            adv[c, i] = adv[c, i] + u * value
        return carry

    lax.fori_loop(0, seg, along_x, 0, unroll=2)

    row = lax.broadcasted_iota(jnp.int32, vel.shape[2:], 0)

    def along_y(i, carry):
        v = vx[1, i + 2]
        for c in range(COMPS):
            field = vx[c, i + 2]
            other = halo[c, i]
            total = None
            for k, weight in enumerate(STENCIL, 1):
                up = pltpu.roll(jnp.where(row < k, other, field), rows - k, 0)
                down = pltpu.roll(jnp.where(row >= rows - k, other, field), k, 0)
                diff = up - down
                total = weight * diff if total is None else total + weight * diff
            adv[c, i] = -(adv[c, i] + v * total)
        return carry

    for part in range(CHUNKS):
        for copy in y_copies[part]:
            copy.wait_recv()
        lax.fori_loop(cuts[part], cuts[part + 1], along_y, 0, unroll=2)
    for pair in y_copies:
        for copy in pair:
            copy.wait_send()


def place_out(adv_in, gx_in, adv_out, gx_out, sem):
    seg = adv_in.shape[1]
    piece = seg // PIECES
    copies = []
    for part in range(PIECES):
        planes = slice(part * piece, (part + 1) * piece)
        for which, (source, target) in enumerate(((adv_in, adv_out), (gx_in, gx_out))):
            copies.append(
                pltpu.make_async_copy(
                    source.at[:, planes], target.at[:, planes], sem.at[which, part]
                )
            )
    for copy in copies:
        copy.start()
    for copy in copies:
        copy.wait()


def on_device(lines, tiles, velocity):
    comps, seg, rows, depth = velocity.shape
    plane = (comps, rows, depth)
    shape = jax.ShapeDtypeStruct(velocity.shape, jnp.float32)
    adv, gx = pl.pallas_call(
        functools.partial(kernel, lines, tiles),
        out_shape=(shape, shape),
        in_specs=[pl.BlockSpec(memory_space=pltpu.HBM)],
        out_specs=(
            pl.BlockSpec(memory_space=pltpu.VMEM),
            pl.BlockSpec(memory_space=pltpu.VMEM),
        ),
        scratch_shapes=[
            pltpu.VMEM((comps, seg + 4, rows, depth), jnp.float32),
            pltpu.VMEM(velocity.shape, jnp.float32),
            pltpu.VMEM((2,) + plane, jnp.float32),
            pltpu.VMEM((2,) + plane, jnp.float32),
            pltpu.SMEM((seg,), jnp.float32),
            pltpu.SemaphoreType.DMA,
            pltpu.SemaphoreType.DMA((2, CHUNKS)),
            pltpu.SemaphoreType.DMA((2, CHUNKS)),
            pltpu.SemaphoreType.DMA((2,)),
            pltpu.SemaphoreType.DMA((2,)),
            pltpu.SemaphoreType.DMA((2,)),
            pltpu.SemaphoreType.DMA((2,)),
        ],
        compiler_params=pltpu.CompilerParams(
            collective_id=0, has_side_effects=True, vmem_limit_bytes=46 * 1024 * 1024
        ),
    )(velocity)
    return pl.pallas_call(
        place_out,
        out_shape=(shape, shape),
        in_specs=[pl.BlockSpec(memory_space=pltpu.VMEM)] * 2,
        out_specs=(pl.BlockSpec(memory_space=pltpu.HBM),) * 2,
        scratch_shapes=[pltpu.SemaphoreType.DMA((2, PIECES))],
        compiler_params=pltpu.CompilerParams(vmem_limit_bytes=24 * 1024 * 1024),
    )(adv, gx)


def solution(mesh):
    spec = P(None, "line", "cross", None)
    return jax.shard_map(
        functools.partial(on_device, mesh.shape["line"], mesh.shape["cross"]),
        mesh=mesh,
        in_specs=(spec,),
        out_specs=(spec, spec),
        check_vma=False,
    )
```

```python
import functools
import math

import jax
import jax.numpy as jnp
from jax import lax
from jax.experimental import pallas as pl
from jax.experimental.pallas import tpu as pltpu
from jax.sharding import PartitionSpec as P

MESH = pl.DeviceIdType.MESH
ALPHA = 1.0 / 3.0
NEAR = 7.0 / 9.0
FAR = 1.0 / 36.0
ROOT = (math.sqrt(1.0 - 4.0 * ALPHA * ALPHA) - 1.0) / (2.0 * ALPHA)
SCALE = 1.0 + ROOT * ROOT
STENCIL = (45.0 / 60.0, -9.0 / 60.0, 1.0 / 60.0)
WIDTH = 3
CHUNKS = 4
CUTS = (0, 28, 50, 60, 64)
COMPS = 3
PIECES = 4


def kernel(
    lines,
    tiles,
    vel,
    adv,
    gx,
    vx,
    halo,
    ends,
    beside,
    power,
    in_sem,
    y_send,
    y_recv,
    x_send,
    x_recv,
    e_send,
    e_recv,
):
    seg = vel.shape[1]
    rows = vel.shape[2]
    cuts = [seg * cut // CUTS[-1] for cut in CUTS]
    line = lax.axis_index("line")
    tile = lax.axis_index("cross")
    ahead = (lax.rem(line + 1, lines), tile)
    behind = (lax.rem(line + lines - 1, lines), tile)
    above = (line, lax.rem(tile + 1, tiles))
    below = (line, lax.rem(tile + tiles - 1, tiles))

    local = pltpu.make_async_copy(vel, vx.at[:, 2 : 2 + seg], in_sem)
    local.start()

    barrier = pltpu.get_barrier_semaphore()
    for device in (above, below, ahead, behind):
        pl.semaphore_signal(barrier, inc=1, device_id=device, device_id_type=MESH)
    pl.semaphore_wait(barrier, 4)

    def remote(src, dst, send, recv, device):
        return pltpu.make_async_remote_copy(
            src_ref=src,
            dst_ref=dst,
            send_sem=send,
            recv_sem=recv,
            device_id=device,
            device_id_type=MESH,
        )

    x_copies = [
        remote(vel.at[:, seg - 2 : seg], vx.at[:, 0:2], x_send.at[0], x_recv.at[0], ahead),
        remote(vel.at[:, 0:2], vx.at[:, seg + 2 : seg + 4], x_send.at[1], x_recv.at[1], behind),
    ]
    for copy in x_copies:
        copy.start()

    y_copies = []
    for part in range(CHUNKS):
        planes = slice(cuts[part], cuts[part + 1])
        head = slice(0, WIDTH)
        tail = slice(rows - WIDTH, rows)
        pair = (
            remote(
                vel.at[:, planes, tail],
                halo.at[:, planes, tail],
                y_send.at[0, part],
                y_recv.at[0, part],
                above,
            ),
            remote(
                vel.at[:, planes, head],
                halo.at[:, planes, head],
                y_send.at[1, part],
                y_recv.at[1, part],
                below,
            ),
        )
        y_copies.append(pair)
    around = (tile == tiles - 1, tile == 0)
    for pair in y_copies:
        for copy, wraps in zip(pair, around):
            pl.when(wraps)(copy.start)

    def fill(i, value):
        power[i] = value
        return value * ROOT

    lax.fori_loop(0, seg, fill, jnp.float32(ROOT))

    local.wait()
    for pair in y_copies:
        for copy, wraps in zip(pair, around):
            pl.when(jnp.logical_not(wraps))(copy.start)
    for copy in x_copies:
        copy.wait()

    zero = jnp.zeros((COMPS,) + vel.shape[2:], jnp.float32)

    def forward(i, before):
        near = vx[:, i + 3] - vx[:, i + 1]
        far = vx[:, i + 4] - vx[:, i]
        now = (NEAR * near + FAR * far) + ROOT * before
        gx[:, i] = now
        return now

    ends[0] = lax.fori_loop(0, seg, forward, zero, unroll=4)

    def backward(k, after):
        i = seg - 1 - k
        now = SCALE * gx[:, i] + ROOT * after
        gx[:, i] = now
        return now

    ends[1] = lax.fori_loop(0, seg, backward, zero, unroll=4)

    e_copies = [
        remote(ends.at[0], beside.at[0], e_send.at[0], e_recv.at[0], ahead),
        remote(ends.at[1], beside.at[1], e_send.at[1], e_recv.at[1], behind),
    ]
    for copy in e_copies:
        copy.start()

    depth = vel.shape[3]

    def along_z(i, carry):
        w = vx[2, i + 2]
        for c in range(COMPS):
            field = vx[c, i + 2]
            total = None
            for k, weight in enumerate(STENCIL, 1):
                diff = pltpu.roll(field, depth - k, 1) - pltpu.roll(field, k, 1)
                total = weight * diff if total is None else total + weight * diff
            adv[c, i] = w * total
        return carry

    lax.fori_loop(0, seg, along_z, 0, unroll=2)

    for copy in e_copies:
        copy.wait()

    gain = SCALE / (1.0 - ROOT * ROOT)
    left = gain * beside[0]
    right = beside[1] + (gain * ROOT) * ends[0] - (gain * ROOT ** (seg + 1)) * beside[0]

    def along_x(i, carry):
        u = vx[0, i + 2]
        for c in range(COMPS):
            value = gx[c, i] + (power[i] * left[c] + power[seg - 1 - i] * right[c])
            gx[c, i] = value
            adv[c, i] = adv[c, i] + u * value
        return carry

    lax.fori_loop(0, seg, along_x, 0, unroll=2)

    row = lax.broadcasted_iota(jnp.int32, vel.shape[2:], 0)

    def along_y(i, carry):
        v = vx[1, i + 2]
        for c in range(COMPS):
            field = vx[c, i + 2]
            other = halo[c, i]
            total = None
            for k, weight in enumerate(STENCIL, 1):
                up = pltpu.roll(jnp.where(row < k, other, field), rows - k, 0)
                down = pltpu.roll(jnp.where(row >= rows - k, other, field), k, 0)
                diff = up - down
                total = weight * diff if total is None else total + weight * diff
            adv[c, i] = -(adv[c, i] + v * total)
        return carry

    for part in range(CHUNKS):
        for copy in y_copies[part]:
            copy.wait_recv()
        lax.fori_loop(cuts[part], cuts[part + 1], along_y, 0, unroll=2)
    for pair in y_copies:
        for copy in pair:
            copy.wait_send()


def place_out(adv_in, gx_in, adv_out, gx_out, sem):
    seg = adv_in.shape[1]
    piece = seg // PIECES
    copies = []
    for part in range(PIECES):
        planes = slice(part * piece, (part + 1) * piece)
        for which, (source, target) in enumerate(((adv_in, adv_out), (gx_in, gx_out))):
            copies.append(
                pltpu.make_async_copy(
                    source.at[:, planes], target.at[:, planes], sem.at[which, part]
                )
            )
    for copy in copies:
        copy.start()
    for copy in copies:
        copy.wait()


def on_device(lines, tiles, velocity):
    comps, seg, rows, depth = velocity.shape
    plane = (comps, rows, depth)
    shape = jax.ShapeDtypeStruct(velocity.shape, jnp.float32)
    adv, gx = pl.pallas_call(
        functools.partial(kernel, lines, tiles),
        out_shape=(shape, shape),
        in_specs=[pl.BlockSpec(memory_space=pltpu.HBM)],
        out_specs=(
            pl.BlockSpec(memory_space=pltpu.VMEM),
            pl.BlockSpec(memory_space=pltpu.VMEM),
        ),
        scratch_shapes=[
            pltpu.VMEM((comps, seg + 4, rows, depth), jnp.float32),
            pltpu.VMEM(velocity.shape, jnp.float32),
            pltpu.VMEM((2,) + plane, jnp.float32),
            pltpu.VMEM((2,) + plane, jnp.float32),
            pltpu.SMEM((seg,), jnp.float32),
            pltpu.SemaphoreType.DMA,
            pltpu.SemaphoreType.DMA((2, CHUNKS)),
            pltpu.SemaphoreType.DMA((2, CHUNKS)),
            pltpu.SemaphoreType.DMA((2,)),
            pltpu.SemaphoreType.DMA((2,)),
            pltpu.SemaphoreType.DMA((2,)),
            pltpu.SemaphoreType.DMA((2,)),
        ],
        compiler_params=pltpu.CompilerParams(
            collective_id=0, has_side_effects=True, vmem_limit_bytes=46 * 1024 * 1024
        ),
    )(velocity)
    return pl.pallas_call(
        place_out,
        out_shape=(shape, shape),
        in_specs=[pl.BlockSpec(memory_space=pltpu.VMEM)] * 2,
        out_specs=(pl.BlockSpec(memory_space=pltpu.HBM),) * 2,
        scratch_shapes=[pltpu.SemaphoreType.DMA((2, PIECES))],
        compiler_params=pltpu.CompilerParams(vmem_limit_bytes=24 * 1024 * 1024),
    )(adv, gx)


def solution(mesh):
    spec = P(None, "line", "cross", None)
    return jax.shard_map(
        functools.partial(on_device, mesh.shape["line"], mesh.shape["cross"]),
        mesh=mesh,
        in_specs=(spec,),
        out_specs=(spec, spec),
        check_vma=False,
    )
```
